32 devices in a mesh: sweep: 4 (over z), lat: 8 (over y, x, core).
Axes of the slice: x: 2, y: 2, z: 4, core: 2. Of those that a mesh axis runs over, the one named last changes fastest.
Arguments:
- traveltime: float32 [2, 32, 128, 384], P(None, 'sweep', 'lat'), may hold values from 0 to 4
- residual: float32 [2, 32, 128, 384], P(None, 'sweep', 'lat'), may hold values from -6 to 6
- slowness: float32 [32, 128, 384], P('sweep', 'lat'), may hold values from 0.3 to 0.6
- attenuation: float32 [32, 128, 384], P('sweep', 'lat'), may hold values from 0.005 to 0.05
- topography: int32 [128, 384], P('lat'), may hold values from 0 to 31, as said below
Outputs:
- adjoint: float32 [2, 32, 128, 384], P(None, 'sweep', 'lat')
- gradient: float32 [32, 128, 384], P('sweep', 'lat')
The draws below stay inside these ranges and needn't reach their ends.
Inputs may be any that keep to these rules, and one draw needn't show every extreme that they name: Apart from two corner columns, topography is a level shared by each aligned strip of 16 columns along the first lateral dimension plus a small rough offset per column, so that whole blocks of planes lie above it; the first column of the grid has topography 32 - 1 and the last column 0.
All inputs are finite; a program needn't handle non-finite values.
Results may differ from the reference program's by a relative error of at most 0.0003.
Values sent between devices are 32-bit elements; how exact they have to be, the bound alone decides.
A program may use at most 64 MiB of HBM per device.

```python
import math
import jax
import jax.numpy as jnp
from jax import lax

SOURCES = 2
COLS_DEV = 16
NY = 384
NX = 128
NZ = 32


def draw_traveltime(key, part):
    key_parity = jax.random.fold_in(key, 21)
    key_value = jax.random.fold_in(key, 22)
    shape = (SOURCES, NZ, NX, NY)
    parity = jax.random.randint(key_parity, (SOURCES, 1, 1, 1), 0, 2)
    row_ids = lax.broadcasted_iota(jnp.int32, shape, 3)
    raised = (row_ids + parity) % 2 == 0
    uniform_part = jax.random.uniform(key_value, shape, jnp.float32)
    high_values = 3.4 + 0.6 * uniform_part
    low_values = 0.6 * uniform_part
    field = jnp.where(raised, high_values, low_values)
    return field.astype(jnp.float32)


def draw_topography(key, part):
    key_base = jax.random.fold_in(key, 11)
    key_bump = jax.random.fold_in(key, 12)
    strips = NX // COLS_DEV
    levels = jax.random.randint(key_base, (strips,), 0, 3 * NZ // 4)
    bumps = jax.random.randint(key_bump, (NX, NY), 0, NZ // 8 + 1)
    field = jnp.repeat(levels, COLS_DEV)[:, None] + bumps
    row_ids = lax.broadcasted_iota(jnp.int32, (NX, NY), 0)
    col_ids = lax.broadcasted_iota(jnp.int32, (NX, NY), 1)
    field = jnp.where((row_ids == 0) & (col_ids == 0), NZ - 1, field)
    field = jnp.where((row_ids == NX - 1) & (col_ids == NY - 1), 0, field)
    return field.astype(jnp.int32)


def block_levels(stream_key, extent, shards, smallest, largest):
    gain, own = 1.0, jax.random.fold_in(stream_key, 6)
    for dim, blocks in shards:
        heights = jnp.exp(jax.random.uniform(jax.random.fold_in(own, dim), (blocks,), jnp.float32, smallest / len(shards), largest / len(shards)))
        gain = gain * jnp.repeat(heights, extent[dim] // blocks).reshape([-1 if axis == dim else 1 for axis in range(len(extent))])
    return gain


def scatter_about(key, shape, width, bound, shards=(), held_as=jnp.bfloat16):
    gain = block_levels(key, shape, shards, -0.22, 0.18) if shards else 1.0
    values = jax.random.normal(key, shape, jnp.float32) * width * gain
    return jnp.minimum(jnp.maximum(values, -bound), bound).astype(held_as)


def setup_inputs(seed: int = 0) -> dict:
    seeds = jax.random.split(jax.random.key(seed), 6)
    traveltime = draw_traveltime(jax.random.fold_in(seeds[5], 71), 0)
    residual = scatter_about(seeds[1], (SOURCES, NZ, NX, NY), 1.0, 6.0, ((1, 4), (2, 8)), jnp.float32)
    slowness = jnp.clip(jnp.exp(math.log(0.6) - 0.6931472 * jax.random.uniform(seeds[2], (NZ, NX, NY), jnp.float32) ** block_levels(seeds[2], (NZ, NX, NY), ((0, 4), (1, 8)), -0.2, 0.2)), 0.3, 0.6)
    attenuation = jnp.clip(jnp.exp(math.log(0.05) - 2.3025851 * jax.random.uniform(seeds[3], (NZ, NX, NY), jnp.float32) ** block_levels(seeds[3], (NZ, NX, NY), ((0, 4), (1, 8)), -0.2, 0.2)), 0.005, 0.05)
    topography = draw_topography(jax.random.fold_in(seeds[5], 71), 0)
    return dict(traveltime=traveltime, residual=residual, slowness=slowness, attenuation=attenuation, topography=topography)


def shift_low(field, along):
    count = field.shape[along]
    padding = jnp.zeros_like(lax.slice_in_dim(field, 0, 1, axis=along))
    return jnp.concatenate([padding, lax.slice_in_dim(field, 0, count - 1, axis=along)], axis=along)


def shift_high(field, along):
    count = field.shape[along]
    padding = jnp.zeros_like(lax.slice_in_dim(field, 0, 1, axis=along))
    return jnp.concatenate([lax.slice_in_dim(field, 1, count, axis=along), padding], axis=along)


def upwind_weights(tau_wide):
    last = tau_wide.ndim - 1
    center = tau_wide[..., 1:-1, :]
    west = jax.nn.softplus(center - tau_wide[..., :-2, :])
    east = jax.nn.softplus(center - tau_wide[..., 2:, :])
    north = jax.nn.softplus(center - shift_low(center, last))
    south = jax.nn.softplus(center - shift_high(center, last))
    return west, east, north, south


def reference(traveltime, residual, slowness, attenuation, topography):
    sources = traveltime.shape[0]

    def advance(previous, inputs):
        tau_plane, source_plane, slow_plane, atten_plane, plane_index = inputs
        tau_wide = jnp.pad(tau_plane, ((0, 0), (1, 1), (0, 0)))
        west, east, north, south = upwind_weights(tau_wide)
        active = (plane_index >= topography).astype(jnp.float32)
        denominator = slow_plane + west + east + north + south + atten_plane
        scale = active / denominator
        current = scale * (source_plane + slow_plane * previous + west * shift_low(previous, 1)
                           + east * shift_high(previous, 1) + north * shift_low(previous, 2)
                           + south * shift_high(previous, 2))
        return current, current

    inputs = (jnp.moveaxis(traveltime, 1, 0), jnp.moveaxis(residual, 1, 0), slowness, attenuation,
              jnp.arange(slowness.shape[0], dtype=jnp.int32))
    start = jnp.zeros((sources, slowness.shape[1], slowness.shape[2]), jnp.float32)
    _, planes_out = lax.scan(advance, start, inputs)
    adjoint = jnp.moveaxis(planes_out, 0, 1)
    gradient = slowness * jnp.sum(adjoint, axis=0)
    return adjoint, gradient
```

```python
import functools

import jax
import jax.numpy as jnp
from jax import lax
from jax.experimental import pallas as pl
from jax.experimental.pallas import tpu as pltpu
from jax.sharding import PartitionSpec as P

MESH = pl.DeviceIdType.MESH
HALO = 8


def kernel(
    n_sweep, n_lat,
    t_ref, r_ref, s_ref, a_ref, topo_ref,
    adj_ref, grad_ref,
    T, R, S, A, TP, C, IN,
    local_sem, halo_send, halo_recv, topo_send, topo_recv, flow_send, flow_recv,
):
    sources, planes, cols, ny = t_ref.shape
    rows = cols + 2 * HALO
    own = pl.ds(HALO, cols)
    sweep = lax.axis_index("sweep")
    lat = lax.axis_index("lat")
    has_left = lat > 0
    has_right = lat < n_lat - 1
    has_up = sweep > 0
    has_down = sweep < n_sweep - 1

    local = [
        pltpu.make_async_copy(t_ref, T.at[:, :, own], local_sem.at[0]),
        pltpu.make_async_copy(s_ref, S.at[:, own], local_sem.at[1]),
        pltpu.make_async_copy(a_ref, A.at[:, own], local_sem.at[2]),
        pltpu.make_async_copy(topo_ref, TP.at[own], local_sem.at[3]),
        pltpu.make_async_copy(r_ref, R.at[:, :, own], local_sem.at[4]),
    ]
    for copy in local:
        copy.start()

    barrier = pltpu.get_barrier_semaphore()
    near = [
        (has_left, sweep, lat - 1),
        (has_right, sweep, lat + 1),
    ]
    for step, ok in ((-1, has_up), (1, has_down)):
        near += [
            (ok, sweep + step, lat),
            (ok & has_left, sweep + step, lat - 1),
            (ok & has_right, sweep + step, lat + 1),
        ]
    for ok, z, x in near:
        @pl.when(ok)
        def _():
            pl.semaphore_signal(barrier, inc=1, device_id=(z, x), device_id_type=MESH)
    peers = sum(ok.astype(jnp.int32) for ok, _, _ in near)
    pl.semaphore_wait(barrier, peers)

    def halo_copies(side, level):
        src = pl.ds(0, HALO) if side == 0 else pl.ds(cols - HALO, HALO)
        dst = pl.ds(HALO + cols, HALO) if side == 0 else pl.ds(0, HALO)
        peer = (sweep, lat - 1) if side == 0 else (sweep, lat + 1)
        pairs = [
            (t_ref.at[:, level, src], T.at[:, level, dst]),
            (s_ref.at[level, src], S.at[level, dst]),
            (a_ref.at[level, src], A.at[level, dst]),
            (r_ref.at[:, level, src], R.at[:, level, dst]),
        ]
        return [
            pltpu.make_async_remote_copy(
                src_ref=x, dst_ref=y,
                send_sem=halo_send.at[side, level, i], recv_sem=halo_recv.at[side, level, i],
                device_id=peer, device_id_type=MESH,
            )
            for i, (x, y) in enumerate(pairs)
        ]

    def topo_copy(side):
        src = pl.ds(0, HALO) if side == 0 else pl.ds(cols - HALO, HALO)
        dst = pl.ds(HALO + cols, HALO) if side == 0 else pl.ds(0, HALO)
        peer = (sweep, lat - 1) if side == 0 else (sweep, lat + 1)
        return pltpu.make_async_remote_copy(
            src_ref=topo_ref.at[src], dst_ref=TP.at[dst],
            send_sem=topo_send.at[side], recv_sem=topo_recv.at[side],
            device_id=peer, device_id_type=MESH,
        )

    sides = ((0, has_left), (1, has_right))
    for side, ok in sides:
        @pl.when(ok)
        def _():
            topo_copy(side).start()

    def send_level(level, carry):
        for side, ok in sides:
            @pl.when(ok)
            def _():
                for copy in halo_copies(side, level):
                    copy.start()
        return carry

    lax.fori_loop(0, planes, send_level, 0)

    for ok, dst in ((has_left, pl.ds(0, HALO)), (has_right, pl.ds(HALO + cols, HALO))):
        @pl.when(jnp.logical_not(ok))
        def _():
            T[:, :, dst] = jnp.zeros((sources, planes, HALO, ny), jnp.float32)
            R[:, :, dst] = jnp.zeros((sources, planes, HALO, ny), jnp.float32)
            S[:, dst] = jnp.zeros((planes, HALO, ny), jnp.float32)
            A[:, dst] = jnp.zeros((planes, HALO, ny), jnp.float32)
            TP[dst] = jnp.full((HALO, ny), n_sweep * planes, jnp.int32)
            IN[:, dst] = jnp.zeros((sources, HALO, ny), jnp.float32)

    @pl.when(jnp.logical_not(has_up))
    def _():
        IN[...] = jnp.zeros((sources, rows, ny), jnp.float32)

    for copy in local:
        copy.wait()
    arrivals = ((0, has_right), (1, has_left))
    for side, ok in arrivals:
        @pl.when(ok)
        def _():
            topo_copy(side).wait_recv()

    lane = lax.broadcasted_iota(jnp.int32, (rows, ny), 1)
    first = lane == 0
    last = lane == ny - 1

    def log_part(d):
        return jnp.log(1.0 + jnp.exp(-jnp.abs(d)))

    def weigh(level, carry):
        for side, ok in arrivals:
            @pl.when(ok)
            def _():
                for copy in halo_copies(side, level):
                    copy.wait_recv()
        slow = S[level]
        base = slow + A[level]
        active = sweep * planes + level >= TP[...]
        for k in range(sources):
            t = T[k, level]
            d = t - pltpu.roll(t, 1, 0)
            p = log_part(d)
            west = jnp.maximum(d, 0.0) + p
            east = pltpu.roll(jnp.maximum(-d, 0.0) + p, rows - 1, 0)
            d = t - jnp.where(first, 0.0, pltpu.roll(t, 1, 1))
            p = log_part(d)
            north = jnp.maximum(d, 0.0) + p
            end = jnp.maximum(t, 0.0) + log_part(t)
            south = jnp.where(last, end, pltpu.roll(jnp.maximum(-d, 0.0) + p, ny - 1, 1))
            scale = jnp.where(active, 1.0 / (base + west + east + north + south), 0.0)
            C[k, level, 0] = scale * R[k, level]
            C[k, level, 1] = scale * slow
            C[k, level, 2] = scale * west
            C[k, level, 3] = scale * east
            C[k, level, 4] = jnp.where(first, 0.0, scale * north)
            C[k, level, 5] = jnp.where(last, 0.0, scale * south)
        return carry

    lax.fori_loop(0, planes, weigh, 0)

    def flow_copies(k):
        low, high = pl.ds(0, HALO), pl.ds(HALO + cols, HALO)
        parts = [
            (pl.ds(0, cols), own, lat),
            (pl.ds(0, HALO), high, lat - 1),
            (pl.ds(cols - HALO, HALO), low, lat + 1),
        ]
        return [
            pltpu.make_async_remote_copy(
                src_ref=adj_ref.at[k, planes - 1, src], dst_ref=IN.at[k, dst],
                send_sem=flow_send.at[k, i], recv_sem=flow_recv.at[k, i],
                device_id=(sweep + 1, x), device_id_type=MESH,
            )
            for i, (src, dst, x) in enumerate(parts)
        ]

    for k in range(sources):
        copies = flow_copies(k)
        for copy, ok in zip(copies, (has_up, has_up & has_right, has_up & has_left)):
            @pl.when(ok)
            def _():
                copy.wait_recv()

        def advance(level, previous):
            current = (
                C[k, level, 0]
                + C[k, level, 1] * previous
                + C[k, level, 2] * pltpu.roll(previous, 1, 0)
                + C[k, level, 3] * pltpu.roll(previous, rows - 1, 0)
                + C[k, level, 4] * pltpu.roll(previous, 1, 1)
                + C[k, level, 5] * pltpu.roll(previous, ny - 1, 1)
            )
            adj_ref[k, level] = current[HALO : HALO + cols]
            return current

        lax.fori_loop(0, planes, advance, IN[k])
        for copy, ok in zip(copies, (has_down, has_down & has_left, has_down & has_right)):
            @pl.when(ok)
            def _():
                copy.start()

    def total(level, carry):
        field = adj_ref[0, level]
        for k in range(1, sources):
            field = field + adj_ref[k, level]
        grad_ref[level] = S[level, own] * field
        return carry

    lax.fori_loop(0, planes, total, 0)

    def drain(level, carry):
        for side, ok in sides:
            @pl.when(ok)
            def _():
                for copy in halo_copies(side, level):
                    copy.wait_send()
        return carry

    lax.fori_loop(0, planes, drain, 0)
    for side, ok in sides:
        @pl.when(ok)
        def _():
            topo_copy(side).wait_send()
    for k in range(sources):
        for copy, ok in zip(flow_copies(k), (has_down, has_down & has_left, has_down & has_right)):
            @pl.when(ok)
            def _():
                copy.wait_send()


def shards(n_sweep, n_lat, traveltime, residual, slowness, attenuation, topography):
    sources, planes, cols, ny = traveltime.shape
    rows = cols + 2 * HALO
    f32 = jnp.float32
    return pl.pallas_call(
        functools.partial(kernel, n_sweep, n_lat),
        out_shape=(
            jax.ShapeDtypeStruct(traveltime.shape, f32),
            jax.ShapeDtypeStruct(slowness.shape, f32),
        ),
        in_specs=[pl.BlockSpec(memory_space=pl.ANY)] * 5,
        out_specs=(pl.BlockSpec(memory_space=pltpu.VMEM),) * 2,
        scratch_shapes=[
            pltpu.VMEM((sources, planes, rows, ny), f32),
            pltpu.VMEM((sources, planes, rows, ny), f32),
            pltpu.VMEM((planes, rows, ny), f32),
            pltpu.VMEM((planes, rows, ny), f32),
            pltpu.VMEM((rows, ny), jnp.int32),
            pltpu.VMEM((sources, planes, 6, rows, ny), f32),
            pltpu.VMEM((sources, rows, ny), f32),
            pltpu.SemaphoreType.DMA((5,)),
            pltpu.SemaphoreType.DMA((2, planes, 4)),
            pltpu.SemaphoreType.DMA((2, planes, 4)),
            pltpu.SemaphoreType.DMA((2,)),
            pltpu.SemaphoreType.DMA((2,)),
            pltpu.SemaphoreType.DMA((sources, 3)),
            pltpu.SemaphoreType.DMA((sources, 3)),
        ],
        compiler_params=pltpu.CompilerParams(
            collective_id=0, has_side_effects=True, vmem_limit_bytes=60 * 1024 * 1024
        ),
    )(traveltime, residual, slowness, attenuation, topography)


def solution(mesh):
    in_specs = (
        P(None, "sweep", "lat", None),
        P(None, "sweep", "lat", None),
        P("sweep", "lat", None),
        P("sweep", "lat", None),
        P("lat", None),
    )
    out_specs = (P(None, "sweep", "lat", None), P("sweep", "lat", None))
    body = functools.partial(shards, mesh.shape["sweep"], mesh.shape["lat"])
    return jax.shard_map(body, mesh=mesh, in_specs=in_specs, out_specs=out_specs, check_vma=False)
```

```python
import functools

import jax
import jax.numpy as jnp
from jax import lax
from jax.experimental import pallas as pl
from jax.experimental.pallas import tpu as pltpu
from jax.sharding import PartitionSpec as P

MESH = pl.DeviceIdType.MESH
HALO = 8


def kernel(
    n_sweep, n_lat,
    t_ref, r_ref, s_ref, a_ref, topo_ref,
    adj_ref, grad_ref,
    T, R, S, A, TP, C, IN,
    local_sem, halo_send, halo_recv, topo_send, topo_recv, flow_send, flow_recv,
):
    sources, planes, cols, ny = t_ref.shape
    rows = cols + 2 * HALO
    own = pl.ds(HALO, cols)
    sweep = lax.axis_index("sweep")
    lat = lax.axis_index("lat")
    has_left = lat > 0
    has_right = lat < n_lat - 1
    has_up = sweep > 0
    has_down = sweep < n_sweep - 1

    local = [
        pltpu.make_async_copy(t_ref, T.at[:, :, own], local_sem.at[0]),
        pltpu.make_async_copy(s_ref, S.at[:, own], local_sem.at[1]),
        pltpu.make_async_copy(a_ref, A.at[:, own], local_sem.at[2]),
        pltpu.make_async_copy(topo_ref, TP.at[own], local_sem.at[3]),
        pltpu.make_async_copy(r_ref, R.at[:, :, own], local_sem.at[4]),
    ]
    for copy in local:
        copy.start()

    barrier = pltpu.get_barrier_semaphore()
    near = [
        (has_left, sweep, lat - 1),
        (has_right, sweep, lat + 1),
    ]
    for step, ok in ((-1, has_up), (1, has_down)):
        near += [
            (ok, sweep + step, lat),
            (ok & has_left, sweep + step, lat - 1),
            (ok & has_right, sweep + step, lat + 1),
        ]
    for ok, z, x in near:
        @pl.when(ok)
        def _():
            pl.semaphore_signal(barrier, inc=1, device_id=(z, x), device_id_type=MESH)
    peers = sum(ok.astype(jnp.int32) for ok, _, _ in near)
    pl.semaphore_wait(barrier, peers)

    def halo_copies(side, level):
        peer = (sweep, lat - 1) if side == 0 else (sweep, lat + 1)

        def ends(n):
            if side == 0:
                return pl.ds(0, n), pl.ds(HALO + cols, n)
            return pl.ds(cols - n, n), pl.ds(HALO - n, n)

        src, dst = ends(HALO - level)
        pairs = [(t_ref.at[:, level, src], T.at[:, level, dst])]
        if level < planes - 1:
            src, dst = ends(HALO - 1 - level)
            pairs += [
                (s_ref.at[level, src], S.at[level, dst]),
                (a_ref.at[level, src], A.at[level, dst]),
                (r_ref.at[:, level, src], R.at[:, level, dst]),
            ]
        return [
            pltpu.make_async_remote_copy(
                src_ref=x, dst_ref=y,
                send_sem=halo_send.at[side, level, i], recv_sem=halo_recv.at[side, level, i],
                device_id=peer, device_id_type=MESH,
            )
            for i, (x, y) in enumerate(pairs)
        ]

    def topo_copy(side):
        src = pl.ds(0, HALO) if side == 0 else pl.ds(cols - HALO, HALO)
        dst = pl.ds(HALO + cols, HALO) if side == 0 else pl.ds(0, HALO)
        peer = (sweep, lat - 1) if side == 0 else (sweep, lat + 1)
        return pltpu.make_async_remote_copy(
            src_ref=topo_ref.at[src], dst_ref=TP.at[dst],
            send_sem=topo_send.at[side], recv_sem=topo_recv.at[side],
            device_id=peer, device_id_type=MESH,
        )

    sides = ((0, has_left), (1, has_right))
    for side, ok in sides:
        @pl.when(ok)
        def _():
            topo_copy(side).start()

    def send_level(level, carry):
        for side, ok in sides:
            @pl.when(ok)
            def _():
                for copy in halo_copies(side, level):
                    copy.start()
        return carry

    for level in range(planes):
        send_level(level, 0)

    for ok, dst in ((has_left, pl.ds(0, HALO)), (has_right, pl.ds(HALO + cols, HALO))):
        @pl.when(jnp.logical_not(ok))
        def _():
            T[:, :, dst] = jnp.zeros((sources, planes, HALO, ny), jnp.float32)
            R[:, :, dst] = jnp.zeros((sources, planes, HALO, ny), jnp.float32)
            S[:, dst] = jnp.zeros((planes, HALO, ny), jnp.float32)
            A[:, dst] = jnp.zeros((planes, HALO, ny), jnp.float32)
            TP[dst] = jnp.full((HALO, ny), n_sweep * planes, jnp.int32)
            IN[:, dst] = jnp.zeros((sources, HALO, ny), jnp.float32)

    @pl.when(jnp.logical_not(has_up))
    def _():
        IN[...] = jnp.zeros((sources, rows, ny), jnp.float32)

    for copy in local:
        copy.wait()
    arrivals = ((0, has_right), (1, has_left))
    for side, ok in arrivals:
        @pl.when(ok)
        def _():
            topo_copy(side).wait_recv()

    lane = lax.broadcasted_iota(jnp.int32, (rows, ny), 1)
    first = lane == 0
    last = lane == ny - 1

    def log_part(d):
        return jnp.log(1.0 + jnp.exp(-jnp.abs(d)))

    def weigh(level, carry):
        for side, ok in arrivals:
            @pl.when(ok)
            def _():
                for copy in halo_copies(side, level):
                    copy.wait_recv()
        slow = S[level]
        base = slow + A[level]
        active = sweep * planes + level >= TP[...]
        for k in range(sources):
            t = T[k, level]
            d = t - pltpu.roll(t, 1, 0)
            p = log_part(d)
            west = jnp.maximum(d, 0.0) + p
            east = pltpu.roll(jnp.maximum(-d, 0.0) + p, rows - 1, 0)
            d = t - jnp.where(first, 0.0, pltpu.roll(t, 1, 1))
            p = log_part(d)
            north = jnp.maximum(d, 0.0) + p
            end = jnp.maximum(t, 0.0) + log_part(t)
            south = jnp.where(last, end, pltpu.roll(jnp.maximum(-d, 0.0) + p, ny - 1, 1))
            scale = jnp.where(active, 1.0 / (base + west + east + north + south), 0.0)
            C[k, level, 0] = scale * R[k, level]
            C[k, level, 1] = scale * slow
            C[k, level, 2] = scale * west
            C[k, level, 3] = scale * east
            C[k, level, 4] = jnp.where(first, 0.0, scale * north)
            C[k, level, 5] = jnp.where(last, 0.0, scale * south)
        return carry

    for level in range(planes):
        weigh(level, 0)

    def flow_copies(k):
        low, high = pl.ds(0, HALO), pl.ds(HALO + cols, HALO)
        parts = [
            (pl.ds(0, cols), own, lat),
            (pl.ds(0, HALO), high, lat - 1),
            (pl.ds(cols - HALO, HALO), low, lat + 1),
        ]
        return [
            pltpu.make_async_remote_copy(
                src_ref=adj_ref.at[k, planes - 1, src], dst_ref=IN.at[k, dst],
                send_sem=flow_send.at[k, i], recv_sem=flow_recv.at[k, i],
                device_id=(sweep + 1, x), device_id_type=MESH,
            )
            for i, (src, dst, x) in enumerate(parts)
        ]

    for k in range(sources):
        copies = flow_copies(k)
        for copy, ok in zip(copies, (has_up, has_up & has_right, has_up & has_left)):
            @pl.when(ok)
            def _():
                copy.wait_recv()

        def advance(level, previous):
            current = (
                C[k, level, 0]
                + C[k, level, 1] * previous
                + C[k, level, 2] * pltpu.roll(previous, 1, 0)
                + C[k, level, 3] * pltpu.roll(previous, rows - 1, 0)
                + C[k, level, 4] * pltpu.roll(previous, 1, 1)
                + C[k, level, 5] * pltpu.roll(previous, ny - 1, 1)
            )
            adj_ref[k, level] = current[HALO : HALO + cols]
            return current

        lax.fori_loop(0, planes, advance, IN[k])
        for copy, ok in zip(copies, (has_down, has_down & has_left, has_down & has_right)):
            @pl.when(ok)
            def _():
                copy.start()

    def total(level, carry):
        field = adj_ref[0, level]
        for k in range(1, sources):
            field = field + adj_ref[k, level]
        grad_ref[level] = S[level, own] * field
        return carry

    lax.fori_loop(0, planes, total, 0)

    def drain(level, carry):
        for side, ok in sides:
            @pl.when(ok)
            def _():
                for copy in halo_copies(side, level):
                    copy.wait_send()
        return carry

    for level in range(planes):
        drain(level, 0)
    for side, ok in sides:
        @pl.when(ok)
        def _():
            topo_copy(side).wait_send()
    for k in range(sources):
        for copy, ok in zip(flow_copies(k), (has_down, has_down & has_left, has_down & has_right)):
            @pl.when(ok)
            def _():
                copy.wait_send()


def shards(n_sweep, n_lat, traveltime, residual, slowness, attenuation, topography):
    sources, planes, cols, ny = traveltime.shape
    rows = cols + 2 * HALO
    f32 = jnp.float32
    return pl.pallas_call(
        functools.partial(kernel, n_sweep, n_lat),
        out_shape=(
            jax.ShapeDtypeStruct(traveltime.shape, f32),
            jax.ShapeDtypeStruct(slowness.shape, f32),
        ),
        in_specs=[pl.BlockSpec(memory_space=pl.ANY)] * 5,
        out_specs=(pl.BlockSpec(memory_space=pltpu.VMEM),) * 2,
        scratch_shapes=[
            pltpu.VMEM((sources, planes, rows, ny), f32),
            pltpu.VMEM((sources, planes, rows, ny), f32),
            pltpu.VMEM((planes, rows, ny), f32),
            pltpu.VMEM((planes, rows, ny), f32),
            pltpu.VMEM((rows, ny), jnp.int32),
            pltpu.VMEM((sources, planes, 6, rows, ny), f32),
            pltpu.VMEM((sources, rows, ny), f32),
            pltpu.SemaphoreType.DMA((5,)),
            pltpu.SemaphoreType.DMA((2, planes, 4)),
            pltpu.SemaphoreType.DMA((2, planes, 4)),
            pltpu.SemaphoreType.DMA((2,)),
            pltpu.SemaphoreType.DMA((2,)),
            pltpu.SemaphoreType.DMA((sources, 3)),
            pltpu.SemaphoreType.DMA((sources, 3)),
        ],
        compiler_params=pltpu.CompilerParams(
            collective_id=0, has_side_effects=True, vmem_limit_bytes=24 * 1024 * 1024
        ),
    )(*[pltpu.with_memory_space_constraint(x, pltpu.HBM) for x in (traveltime, residual, slowness, attenuation, topography)])


def solution(mesh):
    in_specs = (
        P(None, "sweep", "lat", None),
        P(None, "sweep", "lat", None),
        P("sweep", "lat", None),
        P("sweep", "lat", None),
        P("lat", None),
    )
    out_specs = (P(None, "sweep", "lat", None), P("sweep", "lat", None))
    body = functools.partial(shards, mesh.shape["sweep"], mesh.shape["lat"])
    return jax.shard_map(body, mesh=mesh, in_specs=in_specs, out_specs=out_specs, check_vma=False)
```

```python
import functools

import jax
import jax.numpy as jnp
from jax import lax
from jax.experimental import pallas as pl
from jax.experimental.pallas import tpu as pltpu
from jax.sharding import PartitionSpec as P

MESH = pl.DeviceIdType.MESH
HALO = 8


def kernel(
    n_sweep, n_lat,
    t_ref, r_ref, s_ref, a_ref, topo_ref,
    adj_ref, grad_ref,
    T, R, S, A, TP, C, IN,
    local_sem, halo_send, halo_recv, topo_send, topo_recv, mid_send, mid_recv, flow_send, flow_recv,
):
    sources, planes, cols, ny = t_ref.shape
    rows = cols + 2 * HALO
    own = pl.ds(HALO, cols)
    sweep = lax.axis_index("sweep")
    lat = lax.axis_index("lat")
    has_left = lat > 0
    has_right = lat < n_lat - 1
    has_up = sweep > 0
    has_down = sweep < n_sweep - 1

    local = [
        pltpu.make_async_copy(t_ref, T.at[:, :, own], local_sem.at[0]),
        pltpu.make_async_copy(s_ref, S.at[:, own], local_sem.at[1]),
        pltpu.make_async_copy(a_ref, A.at[:, own], local_sem.at[2]),
        pltpu.make_async_copy(topo_ref, TP.at[own], local_sem.at[3]),
        pltpu.make_async_copy(r_ref, R.at[:, :, own], local_sem.at[4]),
    ]
    for copy in local:
        copy.start()

    for ok, dst in ((has_left, pl.ds(0, HALO)), (has_right, pl.ds(HALO + cols, HALO))):
        @pl.when(jnp.logical_not(ok))
        def _():
            IN[:, dst] = jnp.zeros((sources, HALO, ny), jnp.float32)

    @pl.when(jnp.logical_not(has_up))
    def _():
        IN[...] = jnp.zeros((sources, rows, ny), jnp.float32)

    barrier = pltpu.get_barrier_semaphore()
    near = [
        (has_left, sweep, lat - 1),
        (has_right, sweep, lat + 1),
    ]
    for step, ok in ((-1, has_up), (1, has_down)):
        near += [
            (ok, sweep + step, lat),
            (ok & has_left, sweep + step, lat - 1),
            (ok & has_right, sweep + step, lat + 1),
        ]
    for ok, z, x in near:
        @pl.when(ok)
        def _():
            pl.semaphore_signal(barrier, inc=1, device_id=(z, x), device_id_type=MESH)
    peers = sum(ok.astype(jnp.int32) for ok, _, _ in near)
    pl.semaphore_wait(barrier, peers)

    def halo_copies(side, level, depth):
        peer = (sweep, lat - 1) if side == 0 else (sweep, lat + 1)

        def ends(n):
            if side == 0:
                return pl.ds(0, n), pl.ds(HALO + cols, n)
            return pl.ds(cols - n, n), pl.ds(HALO - n, n)

        src, dst = ends(depth - level)
        pairs = [(t_ref.at[:, level, src], T.at[:, level, dst])]
        if level < depth - 1:
            src, dst = ends(depth - 1 - level)
            pairs += [
                (s_ref.at[level, src], S.at[level, dst]),
                (a_ref.at[level, src], A.at[level, dst]),
                (r_ref.at[:, level, src], R.at[:, level, dst]),
            ]
        return [
            pltpu.make_async_remote_copy(
                src_ref=x, dst_ref=y,
                send_sem=halo_send.at[side, level, i], recv_sem=halo_recv.at[side, level, i],
                device_id=peer, device_id_type=MESH,
            )
            for i, (x, y) in enumerate(pairs)
        ]

    half = planes // 2

    def each_halo(tests, level, act):
        for side, ok in tests:
            if level >= half:
                cases = ((ok, planes),)
            else:
                cases = ((ok & has_up, planes), (ok & jnp.logical_not(has_up), half))
            for case, depth in cases:
                @pl.when(case)
                def _():
                    for copy in halo_copies(side, level, depth):
                        act(copy)

    def topo_copy(side):
        src = pl.ds(0, HALO) if side == 0 else pl.ds(cols - HALO, HALO)
        dst = pl.ds(HALO + cols, HALO) if side == 0 else pl.ds(0, HALO)
        peer = (sweep, lat - 1) if side == 0 else (sweep, lat + 1)
        return pltpu.make_async_remote_copy(
            src_ref=topo_ref.at[src], dst_ref=TP.at[dst],
            send_sem=topo_send.at[side], recv_sem=topo_recv.at[side],
            device_id=peer, device_id_type=MESH,
        )

    sides = ((0, has_left), (1, has_right))
    for side, ok in sides:
        @pl.when(ok)
        def _():
            topo_copy(side).start()

    for level in range(planes):
        each_halo(sides, level, lambda copy: copy.start())

    for ok, dst in ((has_left, pl.ds(0, HALO)), (has_right, pl.ds(HALO + cols, HALO))):
        @pl.when(jnp.logical_not(ok))
        def _():
            T[:, :, dst] = jnp.zeros((sources, planes, HALO, ny), jnp.float32)
            R[:, :, dst] = jnp.zeros((sources, planes, HALO, ny), jnp.float32)
            S[:, dst] = jnp.zeros((planes, HALO, ny), jnp.float32)
            A[:, dst] = jnp.zeros((planes, HALO, ny), jnp.float32)
            TP[dst] = jnp.full((HALO, ny), n_sweep * planes, jnp.int32)

    for copy in local:
        copy.wait()
    arrivals = ((0, has_right), (1, has_left))
    for side, ok in arrivals:
        @pl.when(ok)
        def _():
            topo_copy(side).wait_recv()

    lane = lax.broadcasted_iota(jnp.int32, (rows, ny), 1)
    first = lane == 0
    last = lane == ny - 1

    def log_part(d):
        return jnp.log(1.0 + jnp.exp(-jnp.abs(d)))

    def weigh(level):
        each_halo(arrivals, level, lambda copy: copy.wait_recv())
        slow = S[level]
        base = slow + A[level]
        active = sweep * planes + level >= TP[...]
        for k in range(sources):
            t = T[k, level]
            d = t - pltpu.roll(t, 1, 0)
            p = log_part(d)
            west = jnp.maximum(d, 0.0) + p
            east = pltpu.roll(jnp.maximum(-d, 0.0) + p, rows - 1, 0)
            d = t - jnp.where(first, 0.0, pltpu.roll(t, 1, 1))
            p = log_part(d)
            north = jnp.maximum(d, 0.0) + p
            end = jnp.maximum(t, 0.0) + log_part(t)
            south = jnp.where(last, end, pltpu.roll(jnp.maximum(-d, 0.0) + p, ny - 1, 1))
            scale = jnp.where(active, 1.0 / (base + west + east + north + south), 0.0)
            C[k, level, 0] = scale * R[k, level]
            C[k, level, 1] = scale * slow
            C[k, level, 2] = scale * west
            C[k, level, 3] = scale * east
            C[k, level, 4] = jnp.where(first, 0.0, scale * north)
            C[k, level, 5] = jnp.where(last, 0.0, scale * south)

    def stepper(k):
        def advance(level, previous):
            current = (
                C[k, level, 0]
                + C[k, level, 1] * previous
                + C[k, level, 2] * pltpu.roll(previous, 1, 0)
                + C[k, level, 3] * pltpu.roll(previous, rows - 1, 0)
                + C[k, level, 4] * pltpu.roll(previous, 1, 1)
                + C[k, level, 5] * pltpu.roll(previous, ny - 1, 1)
            )
            adj_ref[k, level] = current[HALO : HALO + cols]
            return current

        return advance

    def mid_copy(k, side):
        if side == 0:
            src, dst, x = pl.ds(0, half), pl.ds(HALO + cols, half), lat - 1
        else:
            src, dst, x = pl.ds(cols - half, half), pl.ds(HALO - half, half), lat + 1
        return pltpu.make_async_remote_copy(
            src_ref=adj_ref.at[k, half - 1, src], dst_ref=IN.at[k, dst],
            send_sem=mid_send.at[k, side], recv_sem=mid_recv.at[k, side],
            device_id=(sweep, x), device_id_type=MESH,
        )

    for level in range(half):
        weigh(level)

    @pl.when(jnp.logical_not(has_up))
    def _():
        for k in range(sources):
            zero = jnp.zeros((rows, ny), jnp.float32)
            current = lax.fori_loop(0, half, stepper(k), zero)
            for side, ok in sides:
                @pl.when(ok)
                def _():
                    mid_copy(k, side).start()
            IN[k, own] = current[HALO : HALO + cols]

    for level in range(half, planes):
        weigh(level)

    def flow_copies(k):
        low, high = pl.ds(0, HALO), pl.ds(HALO + cols, HALO)
        parts = [
            (pl.ds(0, cols), own, lat),
            (pl.ds(0, HALO), high, lat - 1),
            (pl.ds(cols - HALO, HALO), low, lat + 1),
        ]
        return [
            pltpu.make_async_remote_copy(
                src_ref=adj_ref.at[k, planes - 1, src], dst_ref=IN.at[k, dst],
                send_sem=flow_send.at[k, i], recv_sem=flow_recv.at[k, i],
                device_id=(sweep + 1, x), device_id_type=MESH,
            )
            for i, (src, dst, x) in enumerate(parts)
        ]

    for k in range(sources):
        copies = flow_copies(k)
        for copy, ok in zip(copies, (has_up, has_up & has_right, has_up & has_left)):
            @pl.when(ok)
            def _():
                copy.wait_recv()

        for side, ok in arrivals:
            @pl.when(ok & jnp.logical_not(has_up))
            def _():
                mid_copy(k, side).wait_recv()

        lax.fori_loop(jnp.where(has_up, 0, half), planes, stepper(k), IN[k])
        for copy, ok in zip(copies, (has_down, has_down & has_left, has_down & has_right)):
            @pl.when(ok)
            def _():
                copy.start()

    def total(level, carry):
        field = adj_ref[0, level]
        for k in range(1, sources):
            field = field + adj_ref[k, level]
        grad_ref[level] = S[level, own] * field
        return carry

    lax.fori_loop(0, planes, total, 0)

    for level in range(planes):
        each_halo(sides, level, lambda copy: copy.wait_send())
    for k in range(sources):
        for side, ok in sides:
            @pl.when(ok & jnp.logical_not(has_up))
            def _():
                mid_copy(k, side).wait_send()
    for side, ok in sides:
        @pl.when(ok)
        def _():
            topo_copy(side).wait_send()
    for k in range(sources):
        for copy, ok in zip(flow_copies(k), (has_down, has_down & has_left, has_down & has_right)):
            @pl.when(ok)
            def _():
                copy.wait_send()


def shards(n_sweep, n_lat, traveltime, residual, slowness, attenuation, topography):
    sources, planes, cols, ny = traveltime.shape
    rows = cols + 2 * HALO
    f32 = jnp.float32
    return pl.pallas_call(
        functools.partial(kernel, n_sweep, n_lat),
        out_shape=(
            jax.ShapeDtypeStruct(traveltime.shape, f32),
            jax.ShapeDtypeStruct(slowness.shape, f32),
        ),
        in_specs=[pl.BlockSpec(memory_space=pl.ANY)] * 5,
        out_specs=(pl.BlockSpec(memory_space=pltpu.VMEM),) * 2,
        scratch_shapes=[
            pltpu.VMEM((sources, planes, rows, ny), f32),
            pltpu.VMEM((sources, planes, rows, ny), f32),
            pltpu.VMEM((planes, rows, ny), f32),
            pltpu.VMEM((planes, rows, ny), f32),
            pltpu.VMEM((rows, ny), jnp.int32),
            pltpu.VMEM((sources, planes, 6, rows, ny), f32),
            pltpu.VMEM((sources, rows, ny), f32),
            pltpu.SemaphoreType.DMA((5,)),
            pltpu.SemaphoreType.DMA((2, planes, 4)),
            pltpu.SemaphoreType.DMA((2, planes, 4)),
            pltpu.SemaphoreType.DMA((2,)),
            pltpu.SemaphoreType.DMA((2,)),
            pltpu.SemaphoreType.DMA((sources, 2)),
            pltpu.SemaphoreType.DMA((sources, 2)),
            pltpu.SemaphoreType.DMA((sources, 3)),
            pltpu.SemaphoreType.DMA((sources, 3)),
        ],
        compiler_params=pltpu.CompilerParams(
            collective_id=0, has_side_effects=True, vmem_limit_bytes=24 * 1024 * 1024
        ),
    )(*[pltpu.with_memory_space_constraint(x, pltpu.HBM) for x in (traveltime, residual, slowness, attenuation, topography)])


def solution(mesh):
    in_specs = (
        P(None, "sweep", "lat", None),
        P(None, "sweep", "lat", None),
        P("sweep", "lat", None),
        P("sweep", "lat", None),
        P("lat", None),
    )
    out_specs = (P(None, "sweep", "lat", None), P("sweep", "lat", None))
    body = functools.partial(shards, mesh.shape["sweep"], mesh.shape["lat"])
    return jax.shard_map(body, mesh=mesh, in_specs=in_specs, out_specs=out_specs, check_vma=False)
```
